256 devices in a mesh: replica: 32 (over y, x, core), fsdp: 8 (over z).
Axes of the slice: x: 4, y: 4, z: 8, core: 2. Of those that a mesh axis runs over, the one named last changes fastest.
Arguments:
- global_weights: float32 [1024, 8192], P('fsdp')
- replica_weights: bfloat16 [32, 1024, 8192], P('replica', 'fsdp')
- exponents: int32 [32, 1024, 64], P('replica', 'fsdp'), may hold values from -14 to -6, as said below
- momentum: float32 [1024, 8192], P('fsdp', 'replica'), may hold values from -0.4375 to 0.4375
Outputs:
- new_weights: float32 [1024, 8192], P('fsdp')
- new_momentum: float32 [1024, 8192], P('fsdp', 'replica')
The draws below stay inside these ranges and needn't reach their ends.
Inputs may be any that keep to these rules, and one draw needn't show every extreme that they name: `exponents`: one exponent for each 128 consecutive columns of each replica's row, set by the block's largest magnitude so that most of its entries fit the code range.
All inputs are finite; a program needn't handle non-finite values.
Results may differ from the reference program's by a relative error of at most 0.0003.
Values sent between devices are 32-bit elements; how exact they have to be, the bound alone decides.
No kernel may reach another device: no remote copies, remote signals or barrier semaphores. Data moves between devices by JAX's collectives and lax.ppermute only.
A program may use at most 64 MiB of HBM per device.

```python
import math
import jax
import jax.numpy as jnp
from jax import lax

COLS = 8192
BLOCK = 128
ROWS = 1024
REPLICAS = 32


def shared_levels(key):
    block_count = COLS // BLOCK
    group_blocks = block_count // REPLICAS
    row_groups = (ROWS + 15) // 16
    column_key, row_key, offset_key, pairing_key = jax.random.split(jax.random.fold_in(key, 100), 4)
    column_level = jax.random.randint(column_key, (1, 1, block_count), 0, 4)
    group_level = jax.random.randint(row_key, (1, row_groups, 1), 0, 3)
    row_level = jnp.repeat(group_level, 16, axis=1)[:, :ROWS, :]
    offsets = jax.random.randint(offset_key, (REPLICAS, ROWS, block_count), 0, 2)
    pairing = jax.random.permutation(pairing_key, REPLICAS)
    groups = jnp.arange(block_count) // group_blocks
    spiked = (groups[None, None, :] == pairing[:, None, None]).astype(jnp.int32)
    return (-14 + column_level + row_level + offsets + 2 * spiked).astype(jnp.int32)


def shared_outer(key):
    bell_key = jax.random.fold_in(jax.random.fold_in(key, 200), 1)
    bell = jnp.clip(jax.random.normal(bell_key, (ROWS, COLS), jnp.float32), -6.0, 6.0)
    return bell


def draw_exponents(key, part):
    return shared_levels(key)


def draw_global_weights(key, part):
    outer = shared_outer(key)
    return outer


def draw_replica_weights(key, part):
    levels = shared_levels(key)
    outer = shared_outer(key)
    key = jax.random.fold_in(key, 2)
    noise_key = jax.random.fold_in(key, 0)
    common_key = jax.random.fold_in(key, 2)
    block_count = COLS // BLOCK
    common = jax.random.uniform(common_key, (ROWS, COLS), jnp.float32, -1.0, 1.0)
    noise = jax.random.uniform(noise_key, (REPLICAS, ROWS, COLS), jnp.float32, -1.0, 1.0)
    mixed = (0.55 * (common[None] + noise)).reshape(REPLICAS, ROWS, block_count, BLOCK)
    difference = (mixed * (448.0 * jnp.exp2(levels.astype(jnp.float32)))[..., None]).reshape(REPLICAS, ROWS, COLS)
    return (outer[None] - difference).astype(jnp.bfloat16)


def level_of(stream_key, dims, cuts, low, top_value):
    level = 1.0
    for axis_at, parts in cuts:
        heights = jax.random.uniform(jax.random.fold_in(jax.random.fold_in(stream_key, 6), axis_at), (parts,), jnp.float32, low / len(cuts), top_value / len(cuts))
        level = level * jnp.repeat(jnp.exp(heights), dims[axis_at] // parts).reshape((-1,) + (1,) * (len(dims) - 1 - axis_at))
    return level


def centred(key, shape, width, limit, cuts=(), kind=jnp.bfloat16):
    result = jax.random.normal(key, shape, jnp.float32) * width
    if len(cuts) > 0:
        result = level_of(key, shape, cuts, -0.22, 0.18) * result
    return jnp.clip(result, min=-limit, max=limit).astype(kind)


def setup_inputs(seed: int = 0) -> dict:
    arg_keys = jax.random.split(jax.random.key(seed), 5)
    global_weights = draw_global_weights(jax.random.fold_in(arg_keys[4], 71), 0)
    replica_weights = draw_replica_weights(jax.random.fold_in(arg_keys[4], 71), 0)
    exponents = draw_exponents(jax.random.fold_in(arg_keys[4], 71), 0)
    momentum = centred(arg_keys[3], (ROWS, COLS), 0.03, 0.4375, ((0, 8), (1, 32)), jnp.float32)
    return {"global_weights": global_weights, "replica_weights": replica_weights, "exponents": exponents, "momentum": momentum}


FP8_LIMIT = 448.0
CLIP_SCALE = 0.03
OUTER_RATE = 0.7
OUTER_MOMENTUM = 0.9

def reference(global_weights, replica_weights, exponents, momentum):
    row_count, col_count = global_weights.shape
    block_count = col_count // BLOCK

    def accumulate(summed, items):
        local_weights, local_exponents = items
        difference = (global_weights - local_weights.astype(jnp.float32)).reshape(row_count, block_count, BLOCK)
        scaled = local_exponents.astype(jnp.float32)
        encoded = jnp.clip(difference * jnp.exp2(-scaled)[..., None], -FP8_LIMIT, FP8_LIMIT)
        decoded = encoded * jnp.exp2(scaled)[..., None]
        return (summed + decoded.reshape(row_count, col_count), None)
    summed, _ = lax.scan(accumulate, jnp.zeros((row_count, col_count), jnp.float32), (replica_weights, exponents))
    average = summed / REPLICAS
    magnitude = jnp.sqrt(jnp.sum(average * average))
    threshold = CLIP_SCALE * math.sqrt(ROWS * COLS)
    factor = jnp.minimum(1.0, threshold / (magnitude + 1e-06))
    outer_grad = average * factor
    new_momentum = OUTER_MOMENTUM * momentum + outer_grad
    new_weights = global_weights - OUTER_RATE * (outer_grad + OUTER_MOMENTUM * new_momentum)
    return (new_weights, new_momentum)
```

```python
import functools
import math

import jax
import jax.numpy as jnp
from jax import lax
from jax.experimental import pallas as pl
from jax.experimental.pallas import tpu as pltpu
from jax.sharding import PartitionSpec as P

BLOCK = 128
SIDE = 4
WIDTH = 256
LOADS = 8
STEPS = (2, 1, 3)

FP8_LIMIT = 448.0
CLIP_SCALE = 0.03
OUTER_RATE = 0.7
OUTER_MOMENTUM = 0.9

VMEM = pl.BlockSpec(memory_space=pltpu.VMEM)
HBM = pl.BlockSpec(memory_space=pltpu.HBM)
SCOPED = 12 * 1024 * 1024


def index_of(y, x, core):
    return (y % SIDE) * 8 + (x % SIDE) * 2 + core


def replica_perm(move):
    return [
        (index_of(y, x, core), index_of(*move(y, x, core)))
        for y in range(SIDE)
        for x in range(SIDE)
        for core in range(2)
    ]


def along_major(move):
    return replica_perm(lambda y, x, c: (y, move(x), c) if c == 0 else (move(y), x, c))


def along_minor(move):
    return replica_perm(lambda y, x, c: (move(y), x, c) if c == 0 else (y, move(x), c))


def major_shift(step):
    return along_major(lambda at: at + step)


def minor_shift(step):
    return along_minor(lambda at: at + step)


CORE_SWAP = replica_perm(lambda y, x, c: (y, x, 1 - c))
EVEN_PAIRS = along_minor(lambda at: at ^ 1)
ODD_PAIRS = along_minor(lambda at: ((at + 3) % 4 ^ 1) + 1)
Z_ROUNDS = [
    [(z, z ^ 1) for z in range(8)],
    [(z, z ^ 2) for z in range(8)],
    [(z, 7 - z) for z in range(8)],
]


def axes_of(me, core):
    x, y = lax.rem(me // 2, SIDE), me // 8
    return jnp.where(core == 0, x, y), jnp.where(core == 0, y, x)


def owner_of(core, major, minor):
    x, y = jnp.where(core == 0, major, minor), jnp.where(core == 0, minor, major)
    return y * 8 + x * 2 + core


def columns_of(owner):
    return pl.ds(pl.multiple_of(owner * WIDTH, WIDTH), WIDTH)


def encode_kernel(weights, local, exponents, momentum, *refs):
    outs, scratch = refs[: 2 * SIDE], refs[2 * SIDE :]
    base, wbuf, lbuf, ebuf, mbuf, limits, wsem, lsem, sem = scratch
    rows = weights.shape[0] // LOADS
    me = lax.axis_index("replica")
    core = lax.rem(me, 2)
    load_exponents = pltpu.make_async_copy(exponents, ebuf, sem.at[0])
    load_exponents.start()
    loads = []
    for n in range(LOADS):
        part = pl.ds(n * rows, rows)
        pair = (
            pltpu.make_async_copy(weights.at[part], wbuf.at[part], wsem.at[n]),
            pltpu.make_async_copy(local.at[part], lbuf.at[part], lsem.at[n]),
        )
        for copy in pair:
            copy.start()
        loads.append(pair)
    load_momentum = pltpu.make_async_copy(momentum, mbuf, sem.at[1])
    load_momentum.start()
    load_exponents.wait()
    tops = (FP8_LIMIT * jnp.exp2(ebuf[...].astype(jnp.float32))).astype(jnp.bfloat16)
    blocks = tops.shape[0]
    row = lax.broadcasted_iota(jnp.int32, (blocks, WIDTH), 0)
    col = lax.broadcasted_iota(jnp.int32, (blocks, WIDTH), 1) // BLOCK
    work = []
    for n, k in enumerate((*STEPS, 0)):
        for keep in range(2):
            for j in range(SIDE):
                target = core if keep else 1 - core
                owner = owner_of(target, lax.rem(axes_of(me, target)[0] + k, SIDE), j)
                pick = jnp.where(row == 2 * owner + col, 1.0, 0.0).astype(jnp.bfloat16)
                limits[len(work)] = lax.dot_general(
                    tops, pick, (((0,), (0,)), ((), ())), preferred_element_type=jnp.float32
                )
                work.append((outs[SIDE * keep + n], j, columns_of(owner)))
    for n in range(LOADS):
        for copy in loads[n]:
            copy.wait()
        part = pl.ds(n * rows, rows)
        for at, (out, slot, columns) in enumerate(work):
            limit = limits[at, part, :]
            difference = wbuf[part, columns] - lbuf[part, columns].astype(jnp.float32)
            out[slot, part, :] = jnp.clip(difference, -limit, limit)
    decay = OUTER_RATE * OUTER_MOMENTUM * OUTER_MOMENTUM
    load_momentum.wait()
    base[...] = wbuf[:, columns_of(me)] - decay * mbuf[...]


def encode(weights, local, exponents, momentum):
    rows, cols = weights.shape
    blocks = [jax.ShapeDtypeStruct((SIDE, rows, WIDTH), jnp.float32)] * SIDE
    outs = pl.pallas_call(
        encode_kernel,
        out_shape=[*blocks, *blocks, jax.ShapeDtypeStruct((rows, WIDTH), jnp.float32)],
        in_specs=[HBM] * 4,
        out_specs=[VMEM] * (2 * SIDE + 1),
        scratch_shapes=[
            pltpu.VMEM((rows, cols), jnp.float32),
            pltpu.VMEM((rows, cols), jnp.bfloat16),
            pltpu.VMEM(exponents.shape, jnp.int32),
            pltpu.VMEM(momentum.shape, jnp.float32),
            pltpu.VMEM((2 * SIDE * SIDE, rows, WIDTH), jnp.float32),
            pltpu.SemaphoreType.DMA((LOADS,)),
            pltpu.SemaphoreType.DMA((LOADS,)),
            pltpu.SemaphoreType.DMA((2,)),
        ],
        compiler_params=pltpu.CompilerParams(vmem_limit_bytes=SCOPED),
        cost_estimate=pl.CostEstimate(flops=2**22, bytes_accessed=6 * 2**20, transcendentals=0),
        name="encode",
    )(*(pltpu.with_memory_space_constraint(x, pltpu.HBM) for x in (weights, local, exponents, momentum)))
    return outs[:SIDE], outs[SIDE : 2 * SIDE], outs[2 * SIDE]


def squares_kernel(values, out):
    total = None
    for r in range(0, values.shape[0], 8):
        value = values[r : r + 8, :]
        total = value * value if total is None else total + value * value
    out[...] = total


def sum_squares(values):
    return pl.pallas_call(
        squares_kernel,
        out_shape=jax.ShapeDtypeStruct((8, WIDTH), jnp.float32),
        in_specs=[VMEM],
        out_specs=VMEM,
        compiler_params=pltpu.CompilerParams(vmem_limit_bytes=SCOPED),
        cost_estimate=pl.CostEstimate(flops=2**18, bytes_accessed=2**12, transcendentals=0),
        name="squares",
    )(values)


def update_kernel(threshold, *refs):
    mine, handed, (momentum, new_momentum, out, buf, sem) = refs[:5], refs[5:13], refs[13:]
    rows = momentum.shape[0]
    size, half = SIDE * rows, rows // 2
    me = lax.axis_index("replica")
    core = lax.rem(me, 2)
    squares = mine[-1][size:, :] + handed[-1][size:, :]
    magnitude = jnp.sqrt(jnp.sum(squares, axis=(0, 1), keepdims=True))
    factor = jnp.minimum(1.0, threshold / (magnitude + 1e-06))
    rate = OUTER_RATE * (1.0 + OUTER_MOMENTUM) * factor
    own = [(k, mine[n], 0, mine[n], size) for n, k in enumerate((0, 1, 3))]
    own.append((2, mine[3], 0, mine[4], 0))
    other = [(k, handed[2 * n], 0, handed[2 * n + 1], 0) for n, k in enumerate((0, 1, 3, 2))]
    copies = []
    for side, sources in ((core, own), (1 - core, other)):
        major, minor = axes_of(me, side)
        for k, averages, first, bases, offset in sources:
            place = lax.rem(major + SIDE - k, SIDE)
            for j in range(SIDE):
                apart = minor ^ j
                low = jnp.where(apart < 2, apart, 5 - apart)
                high = jnp.where(apart == 0, 0, lax.rem(apart, SIDE - 1) + 1)
                at = len(copies)
                for n, slot in enumerate((low, SIDE + high)):
                    base = pl.ds(pl.multiple_of(offset + slot * half, half), half)
                    average = averages[first + j * rows + n * half : first + j * rows + (n + 1) * half, :]
                    buf[at, n * half : (n + 1) * half, :] = bases[base, :] - rate * average
                columns = columns_of(owner_of(side, place, j))
                copy = pltpu.make_async_copy(buf.at[at], out.at[:, columns], sem.at[at])
                copy.start()
                copies.append(copy)
    here = pl.ds(pl.multiple_of(axes_of(me, core)[1] * rows, rows), rows)
    new_momentum[...] = OUTER_MOMENTUM * momentum[...] + factor * mine[0][here, :]
    for copy in copies:
        copy.wait()


def update(cols, threshold, mine, handed, momentum):
    rows = momentum.shape[0]
    chunks = 2 * SIDE * SIDE
    return pl.pallas_call(
        functools.partial(update_kernel, threshold),
        out_shape=[
            jax.ShapeDtypeStruct((rows, WIDTH), jnp.float32),
            jax.ShapeDtypeStruct((rows, cols), jnp.float32),
        ],
        in_specs=[VMEM] * (len(mine) + len(handed) + 1),
        out_specs=[VMEM, HBM],
        scratch_shapes=[
            pltpu.VMEM((chunks, rows, WIDTH), jnp.float32),
            pltpu.SemaphoreType.DMA((chunks,)),
        ],
        compiler_params=pltpu.CompilerParams(vmem_limit_bytes=SCOPED),
        cost_estimate=pl.CostEstimate(flops=2**21, bytes_accessed=2**22, transcendentals=0),
        name="update",
    )(*mine, *handed, momentum)


def tie(*values):
    return lax.optimization_barrier(values)


def per_device(global_weights, replica_weights, exponents, momentum):
    replica_count = lax.axis_size("replica")
    row_count, col_count = global_weights.shape
    threshold = CLIP_SCALE * math.sqrt(row_count * lax.axis_size("fsdp") * col_count)
    up, down = major_shift(1), major_shift(-1)

    def move(value, perm):
        return lax.ppermute(value, "replica", perm)

    with jax.named_scope("core_sum"):
        send, keep, base = encode(global_weights, replica_weights[0], exponents[0].T, momentum)
        parts = [kept + move(sent, CORE_SWAP) for sent, kept in zip(send, keep)]

    with jax.named_scope("major_sum"):
        arrived = [move(part, major_shift(k)) for part, k in zip(parts, STEPS)]
        total = parts[SIDE - 1] + arrived[0] + arrived[1] + arrived[2]
        low, high = total[:2], total[2:]

    with jax.named_scope("minor_sum"):
        size = low.shape[0] * row_count
        low, high = low.reshape(size, WIDTH), high.reshape(size, WIDTH)
        low_base, high_base = base[: row_count // 2], base[row_count // 2 :]
        for low_perm, high_perm in ((EVEN_PAIRS, ODD_PAIRS), (ODD_PAIRS, EVEN_PAIRS)):
            low_moved = move(jnp.concatenate([low, low_base]), low_perm)
            high_moved = move(jnp.concatenate([high, high_base]), high_perm)
            low, low_base = low + low_moved[:size], jnp.concatenate([low_base, low_moved[size:]])
            high, high_base = high + high_moved[:size], jnp.concatenate([high_base, high_moved[size:]])
        averages = jnp.concatenate([low, high]) / replica_count
        mine = jnp.concatenate([averages, low_base, high_base])
        middle = averages.shape[0]

    with jax.named_scope("square_sum"):
        squares = sum_squares(averages)
        squares = squares + lax.ppermute(squares, "fsdp", Z_ROUNDS[0])
        for perm in Z_ROUNDS[1:]:
            squares = squares + lax.ppermute(squares, "fsdp", perm)

    with jax.named_scope("major_gather"):
        below, above = move(mine, up), move(mine, down)

    with jax.named_scope("major_forward"):
        below, above, squares = tie(below, above, squares)
        far_low = move(jnp.concatenate([below[:middle], squares]), up)
        far_high = move(jnp.concatenate([above[middle:], squares]), down)

    with jax.named_scope("core_gather"):
        whole = tie(mine, squares)[0], below, above
        near = [move(part, CORE_SWAP) for x in whole for part in (x[:middle], x[middle:])]

    with jax.named_scope("square_sum"):
        across = move(squares, major_shift(2))
        far_low, far_high, near = tie(far_low, far_high, near)
        squares = squares + across + far_low[middle:] + far_high[middle:]

    with jax.named_scope("update"):
        (far_low,) = tie(far_low[:middle])
        far_high = jnp.concatenate([far_high[:middle], squares])
        handed = [*near, move(far_low, CORE_SWAP), move(far_high, CORE_SWAP)]
        new_momentum, new_weights = update(
            col_count, threshold, [mine, below, above, far_low, far_high], handed, momentum
        )
    return (new_weights, new_momentum)


def solution(mesh):
    in_specs = (
        P("fsdp", None),
        P("replica", "fsdp", None),
        P("replica", "fsdp", None),
        P("fsdp", "replica"),
    )
    out_specs = (P("fsdp", None), P("fsdp", "replica"))
    return jax.shard_map(
        per_device, mesh=mesh, in_specs=in_specs, out_specs=out_specs, check_vma=False
    )
```

```python
import functools
import math

import jax
import jax.numpy as jnp
from jax import lax
from jax.experimental import pallas as pl
from jax.experimental.pallas import tpu as pltpu
from jax.sharding import PartitionSpec as P

BLOCK = 128
SIDE = 4
WIDTH = 256
LOADS = 8
STEPS = (2, 1, 3)

FP8_LIMIT = 448.0
CLIP_SCALE = 0.03
OUTER_RATE = 0.7
OUTER_MOMENTUM = 0.9

VMEM = pl.BlockSpec(memory_space=pltpu.VMEM)
HBM = pl.BlockSpec(memory_space=pltpu.HBM)
SCOPED = 12 * 1024 * 1024


def index_of(y, x, core):
    return (y % SIDE) * 8 + (x % SIDE) * 2 + core


def replica_perm(move):
    return [
        (index_of(y, x, core), index_of(*move(y, x, core)))
        for y in range(SIDE)
        for x in range(SIDE)
        for core in range(2)
    ]


def along_major(move):
    return replica_perm(lambda y, x, c: (y, move(x), c) if c == 0 else (move(y), x, c))


def along_minor(move):
    return replica_perm(lambda y, x, c: (move(y), x, c) if c == 0 else (y, move(x), c))


def major_shift(step):
    return along_major(lambda at: at + step)


def minor_shift(step):
    return along_minor(lambda at: at + step)


CORE_SWAP = replica_perm(lambda y, x, c: (y, x, 1 - c))
EVEN_PAIRS = along_minor(lambda at: at ^ 1)
ODD_PAIRS = along_minor(lambda at: ((at + 3) % 4 ^ 1) + 1)
Z_ROUNDS = [
    [(z, z ^ 1) for z in range(8)],
    [(z, z ^ 2) for z in range(8)],
    [(z, 7 - z) for z in range(8)],
]


def axes_of(me, core):
    x, y = lax.rem(me // 2, SIDE), me // 8
    return jnp.where(core == 0, x, y), jnp.where(core == 0, y, x)


def owner_of(core, major, minor):
    x, y = jnp.where(core == 0, major, minor), jnp.where(core == 0, minor, major)
    return y * 8 + x * 2 + core


def columns_of(owner):
    return pl.ds(pl.multiple_of(owner * WIDTH, WIDTH), WIDTH)


def encode_kernel(weights, local, exponents, momentum, *refs):
    outs, scratch = refs[: 2 * SIDE], refs[2 * SIDE :]
    base, wbuf, lbuf, ebuf, mbuf, limits, wsem, lsem, sem = scratch
    rows = weights.shape[0] // LOADS
    me = lax.axis_index("replica")
    core = lax.rem(me, 2)
    load_exponents = pltpu.make_async_copy(exponents, ebuf, sem.at[0])
    load_exponents.start()
    loads = []
    for n in range(LOADS):
        part = pl.ds(n * rows, rows)
        pair = (
            pltpu.make_async_copy(weights.at[part], wbuf.at[part], wsem.at[n]),
            pltpu.make_async_copy(local.at[part], lbuf.at[part], lsem.at[n]),
        )
        for copy in pair:
            copy.start()
        loads.append(pair)
    load_momentum = pltpu.make_async_copy(momentum, mbuf, sem.at[1])
    load_momentum.start()
    load_exponents.wait()
    tops = (FP8_LIMIT * jnp.exp2(ebuf[...].astype(jnp.float32))).astype(jnp.bfloat16)
    blocks = tops.shape[0]
    row = lax.broadcasted_iota(jnp.int32, (blocks, WIDTH), 0)
    col = lax.broadcasted_iota(jnp.int32, (blocks, WIDTH), 1) // BLOCK
    work = []
    for n, k in enumerate((*STEPS, 0)):
        for keep in range(2):
            for j in range(SIDE):
                target = core if keep else 1 - core
                owner = owner_of(target, lax.rem(axes_of(me, target)[0] + k, SIDE), j)
                pick = jnp.where(row == 2 * owner + col, 1.0, 0.0).astype(jnp.bfloat16)
                limits[len(work)] = lax.dot_general(
                    tops, pick, (((0,), (0,)), ((), ())), preferred_element_type=jnp.float32
                )
                work.append((outs[SIDE * keep + n], j, columns_of(owner)))
    for n in range(LOADS):
        for copy in loads[n]:
            copy.wait()
        part = pl.ds(n * rows, rows)
        for at, (out, slot, columns) in enumerate(work):
            limit = limits[at, part, :]
            difference = wbuf[part, columns] - lbuf[part, columns].astype(jnp.float32)
            out[slot, part, :] = jnp.clip(difference, -limit, limit)
    decay = OUTER_RATE * OUTER_MOMENTUM * OUTER_MOMENTUM
    load_momentum.wait()
    base[...] = wbuf[:, columns_of(me)] - decay * mbuf[...]


def encode(weights, local, exponents, momentum):
    rows, cols = weights.shape
    blocks = [jax.ShapeDtypeStruct((SIDE, rows, WIDTH), jnp.float32)] * SIDE
    outs = pl.pallas_call(
        encode_kernel,
        out_shape=[*blocks, *blocks, jax.ShapeDtypeStruct((rows, WIDTH), jnp.float32)],
        in_specs=[HBM] * 4,
        out_specs=[VMEM] * (2 * SIDE + 1),
        scratch_shapes=[
            pltpu.VMEM((rows, cols), jnp.float32),
            pltpu.VMEM((rows, cols), jnp.bfloat16),
            pltpu.VMEM(exponents.shape, jnp.int32),
            pltpu.VMEM(momentum.shape, jnp.float32),
            pltpu.VMEM((2 * SIDE * SIDE, rows, WIDTH), jnp.float32),
            pltpu.SemaphoreType.DMA((LOADS,)),
            pltpu.SemaphoreType.DMA((LOADS,)),
            pltpu.SemaphoreType.DMA((2,)),
        ],
        compiler_params=pltpu.CompilerParams(vmem_limit_bytes=SCOPED),
        cost_estimate=pl.CostEstimate(flops=2**22, bytes_accessed=6 * 2**20, transcendentals=0),
        name="encode",
    )(*(pltpu.with_memory_space_constraint(x, pltpu.HBM) for x in (weights, local, exponents, momentum)))
    return outs[:SIDE], outs[SIDE : 2 * SIDE], outs[2 * SIDE]


def squares_kernel(values, out):
    total = None
    for r in range(0, values.shape[0], 8):
        value = values[r : r + 8, :]
        total = value * value if total is None else total + value * value
    out[...] = total


def sum_squares(values):
    return pl.pallas_call(
        squares_kernel,
        out_shape=jax.ShapeDtypeStruct((8, WIDTH), jnp.float32),
        in_specs=[VMEM],
        out_specs=VMEM,
        compiler_params=pltpu.CompilerParams(vmem_limit_bytes=SCOPED),
        cost_estimate=pl.CostEstimate(flops=2**18, bytes_accessed=2**12, transcendentals=0),
        name="squares",
    )(values)


def update_kernel(threshold, steps, first, *refs):
    own_count, other_count = (5, 2 * len(steps)) if first else (0, 2)
    mine, handed = refs[:own_count], refs[own_count : own_count + other_count]
    own_squares, other_squares, last = refs[own_count + other_count :][:3]
    out, buf, sem = refs[-3:]
    rows = buf.shape[1]
    size, half = SIDE * rows, rows // 2
    me = lax.axis_index("replica")
    core = lax.rem(me, 2)
    squares = own_squares[...] + other_squares[...]
    magnitude = jnp.sqrt(jnp.sum(squares, axis=(0, 1), keepdims=True))
    factor = jnp.minimum(1.0, threshold / (magnitude + 1e-06))
    rate = OUTER_RATE * (1.0 + OUTER_MOMENTUM) * factor
    own = []
    if first:
        own = [(k, mine[n], mine[n], size) for n, k in enumerate((0, 1, 3))] + [(2, mine[3], mine[4], 0)]
    other = [(k, handed[2 * n], handed[2 * n + 1], 0) for n, k in enumerate(steps)]
    copies = []
    for side, sources in ((core, own), (1 - core, other)):
        major, minor = axes_of(me, side)
        for k, averages, bases, offset in sources:
            place = lax.rem(major + SIDE - k, SIDE)
            for j in range(SIDE):
                apart = minor ^ j
                low = jnp.where(apart < 2, apart, 5 - apart)
                high = jnp.where(apart == 0, 0, lax.rem(apart, SIDE - 1) + 1)
                at = len(copies)
                for n, slot in enumerate((low, SIDE + high)):
                    base = pl.ds(pl.multiple_of(offset + slot * half, half), half)
                    average = averages[j * rows + n * half : j * rows + (n + 1) * half, :]
                    buf[at, n * half : (n + 1) * half, :] = bases[base, :] - rate * average
                columns = columns_of(owner_of(side, place, j))
                copy = pltpu.make_async_copy(buf.at[at], out.at[:, columns], sem.at[at])
                copy.start()
                copies.append(copy)
    if first:
        momentum, new_momentum = last, refs[-4]
        here = pl.ds(pl.multiple_of(axes_of(me, core)[1] * rows, rows), rows)
        new_momentum[...] = OUTER_MOMENTUM * momentum[...] + factor * mine[0][here, :]
    for copy in copies:
        copy.wait()


def update(rows, cols, threshold, steps, mine, handed, squares, momentum=None, out=None):
    first = out is None
    chunks = SIDE * ((SIDE if first else 0) + len(steps))
    arrays = [*mine, *handed, *squares]
    out_shape = [jax.ShapeDtypeStruct((rows, WIDTH), jnp.float32)] if first else []
    return pl.pallas_call(
        functools.partial(update_kernel, threshold, steps, first),
        out_shape=[*out_shape, jax.ShapeDtypeStruct((rows, cols), jnp.float32)],
        in_specs=[VMEM] * len(arrays) + [VMEM if first else HBM],
        out_specs=([VMEM] if first else []) + [HBM],
        scratch_shapes=[
            pltpu.VMEM((chunks, rows, WIDTH), jnp.float32),
            pltpu.SemaphoreType.DMA((chunks,)),
        ],
        input_output_aliases={} if first else {len(arrays): 0},
        compiler_params=pltpu.CompilerParams(vmem_limit_bytes=SCOPED),
        cost_estimate=pl.CostEstimate(flops=2**16 * chunks, bytes_accessed=2**17 * chunks, transcendentals=0),
        name="update",
    )(*arrays, momentum if first else out)


def tie(*values):
    return lax.optimization_barrier(values)


def per_device(global_weights, replica_weights, exponents, momentum):
    replica_count = lax.axis_size("replica")
    row_count, col_count = global_weights.shape
    threshold = CLIP_SCALE * math.sqrt(row_count * lax.axis_size("fsdp") * col_count)
    up, down = major_shift(1), major_shift(-1)

    def move(value, perm):
        return lax.ppermute(value, "replica", perm)

    with jax.named_scope("core_sum"):
        send, keep, base = encode(global_weights, replica_weights[0], exponents[0].T, momentum)
        parts = [kept + move(sent, CORE_SWAP) for sent, kept in zip(send, keep)]

    with jax.named_scope("major_sum"):
        arrived = [move(part, major_shift(k)) for part, k in zip(parts, STEPS)]
        total = parts[SIDE - 1] + arrived[0] + arrived[1] + arrived[2]
        low, high = total[:2], total[2:]

    with jax.named_scope("minor_sum"):
        size = low.shape[0] * row_count
        low, high = low.reshape(size, WIDTH), high.reshape(size, WIDTH)
        low_base, high_base = base[: row_count // 2], base[row_count // 2 :]
        for low_perm, high_perm in ((EVEN_PAIRS, ODD_PAIRS), (ODD_PAIRS, EVEN_PAIRS)):
            low_moved = move(jnp.concatenate([low, low_base]), low_perm)
            high_moved = move(jnp.concatenate([high, high_base]), high_perm)
            low, low_base = low + low_moved[:size], jnp.concatenate([low_base, low_moved[size:]])
            high, high_base = high + high_moved[:size], jnp.concatenate([high_base, high_moved[size:]])
        averages = jnp.concatenate([low, high]) / replica_count
        mine = jnp.concatenate([averages, low_base, high_base])
        middle = averages.shape[0]

    with jax.named_scope("square_sum"):
        squares = sum_squares(averages)
        squares = squares + lax.ppermute(squares, "fsdp", Z_ROUNDS[0])
        for perm in Z_ROUNDS[1:]:
            squares = squares + lax.ppermute(squares, "fsdp", perm)

    with jax.named_scope("major_gather"):
        below, above = move(mine, up), move(mine, down)

    with jax.named_scope("major_forward"):
        below, above, squares = tie(below, above, squares)
        far_low = move(jnp.concatenate([below[:middle], squares]), up)
        far_high = move(jnp.concatenate([above[middle:], squares]), down)

    with jax.named_scope("core_gather"):
        whole = tie(mine, squares)[0], below, above
        near = [move(part, CORE_SWAP) for x in whole for part in (x[:middle], x[middle:])]

    with jax.named_scope("square_sum"):
        across = move(tie(squares, near[1])[0], major_shift(2))
        far_low, far_high, near, across = tie(far_low, far_high, near, across)
        squares = squares + across + far_low[middle:] + far_high[middle:]

    with jax.named_scope("update"):
        squares = squares, move(squares, CORE_SWAP)
        far = tie(far_low[:middle], far_high[:middle])
        ready = tie(*far, *squares)[:2]
        handed = [move(x, CORE_SWAP) for x in ready]
        new_momentum, new_weights = update(
            row_count, col_count, threshold, (0, 1, 3), [mine, below, above, *far], near, squares, momentum
        )
        (new_weights,) = update(
            row_count, col_count, threshold, (2,), [], handed, squares, None, new_weights
        )
    return (new_weights, new_momentum)


def solution(mesh):
    in_specs = (
        P("fsdp", None),
        P("replica", "fsdp", None),
        P("replica", "fsdp", None),
        P("fsdp", "replica"),
    )
    out_specs = (P("fsdp", None), P("fsdp", "replica"))
    return jax.shard_map(
        per_device, mesh=mesh, in_specs=in_specs, out_specs=out_specs, check_vma=False
    )
```

```python
import functools
import math

import jax
import jax.numpy as jnp
from jax import lax
from jax.experimental import pallas as pl
from jax.experimental.pallas import tpu as pltpu
from jax.sharding import PartitionSpec as P

BLOCK = 128
SIDE = 4
WIDTH = 256
LOADS = 2
STEPS = (2, 1, 3)

FP8_LIMIT = 448.0
CLIP_SCALE = 0.03
OUTER_RATE = 0.7
OUTER_MOMENTUM = 0.9

VMEM = pl.BlockSpec(memory_space=pltpu.VMEM)
HBM = pl.BlockSpec(memory_space=pltpu.HBM)
SCOPED = 12 * 1024 * 1024


def index_of(y, x, core):
    return (y % SIDE) * 8 + (x % SIDE) * 2 + core


def replica_perm(move):
    return [
        (index_of(y, x, core), index_of(*move(y, x, core)))
        for y in range(SIDE)
        for x in range(SIDE)
        for core in range(2)
    ]


def along_major(move):
    return replica_perm(lambda y, x, c: (y, move(x), c) if c == 0 else (move(y), x, c))


def along_minor(move):
    return replica_perm(lambda y, x, c: (move(y), x, c) if c == 0 else (y, move(x), c))


def major_shift(step):
    return along_major(lambda at: at + step)


def minor_shift(step):
    return along_minor(lambda at: at + step)


CORE_SWAP = replica_perm(lambda y, x, c: (y, x, 1 - c))
EVEN_PAIRS = along_minor(lambda at: at ^ 1)
ODD_PAIRS = along_minor(lambda at: ((at + 3) % 4 ^ 1) + 1)
Z_ROUNDS = [
    [(z, z ^ 1) for z in range(8)],
    [(z, z ^ 2) for z in range(8)],
    [(z, 7 - z) for z in range(8)],
]


def axes_of(me, core):
    x, y = lax.rem(me // 2, SIDE), me // 8
    return jnp.where(core == 0, x, y), jnp.where(core == 0, y, x)


def owner_of(core, major, minor):
    x, y = jnp.where(core == 0, major, minor), jnp.where(core == 0, minor, major)
    return y * 8 + x * 2 + core


def columns_of(owner):
    return pl.ds(pl.multiple_of(owner * WIDTH, WIDTH), WIDTH)


def encode_kernel(weights, local, exponents, momentum, *refs):
    outs, scratch = refs[: 2 * SIDE], refs[2 * SIDE :]
    base, wbuf, lbuf, ebuf, mbuf, limits, wsem, lsem, sem = scratch
    rows = weights.shape[0] // LOADS
    me = lax.axis_index("replica")
    core = lax.rem(me, 2)
    load_exponents = pltpu.make_async_copy(exponents, ebuf, sem.at[0])
    load_exponents.start()
    loads = []
    for n in range(LOADS):
        part = pl.ds(n * rows, rows)
        pair = (
            pltpu.make_async_copy(weights.at[part], wbuf.at[part], wsem.at[n]),
            pltpu.make_async_copy(local.at[part], lbuf.at[part], lsem.at[n]),
        )
        for copy in pair:
            copy.start()
        loads.append(pair)
    load_momentum = pltpu.make_async_copy(momentum, mbuf, sem.at[1])
    load_momentum.start()
    load_exponents.wait()
    tops = (FP8_LIMIT * jnp.exp2(ebuf[...].astype(jnp.float32))).astype(jnp.bfloat16)
    blocks = tops.shape[0]
    row = lax.broadcasted_iota(jnp.int32, (blocks, WIDTH), 0)
    col = lax.broadcasted_iota(jnp.int32, (blocks, WIDTH), 1) // BLOCK
    work = []
    for n, k in enumerate((*STEPS, 0)):
        for keep in range(2):
            for j in range(SIDE):
                target = core if keep else 1 - core
                owner = owner_of(target, lax.rem(axes_of(me, target)[0] + k, SIDE), j)
                pick = jnp.where(row == 2 * owner + col, 1.0, 0.0).astype(jnp.bfloat16)
                limits[len(work)] = lax.dot_general(
                    tops, pick, (((0,), (0,)), ((), ())), preferred_element_type=jnp.float32
                )
                work.append((outs[SIDE * keep + n], j, columns_of(owner)))
    for n in range(LOADS):
        for copy in loads[n]:
            copy.wait()
        part = pl.ds(n * rows, rows)
        for at, (out, slot, columns) in enumerate(work):
            limit = limits[at, part, :]
            difference = wbuf[part, columns] - lbuf[part, columns].astype(jnp.float32)
            out[slot, part, :] = jnp.clip(difference, -limit, limit)
    decay = OUTER_RATE * OUTER_MOMENTUM * OUTER_MOMENTUM
    load_momentum.wait()
    base[...] = wbuf[:, columns_of(me)] - decay * mbuf[...]


def encode(weights, local, exponents, momentum):
    rows, cols = weights.shape
    blocks = [jax.ShapeDtypeStruct((SIDE, rows, WIDTH), jnp.float32)] * SIDE
    outs = pl.pallas_call(
        encode_kernel,
        out_shape=[*blocks, *blocks, jax.ShapeDtypeStruct((rows, WIDTH), jnp.float32)],
        in_specs=[HBM] * 4,
        out_specs=[VMEM] * (2 * SIDE + 1),
        scratch_shapes=[
            pltpu.VMEM((rows, cols), jnp.float32),
            pltpu.VMEM((rows, cols), jnp.bfloat16),
            pltpu.VMEM(exponents.shape, jnp.int32),
            pltpu.VMEM(momentum.shape, jnp.float32),
            pltpu.VMEM((2 * SIDE * SIDE, rows, WIDTH), jnp.float32),
            pltpu.SemaphoreType.DMA((LOADS,)),
            pltpu.SemaphoreType.DMA((LOADS,)),
            pltpu.SemaphoreType.DMA((2,)),
        ],
        compiler_params=pltpu.CompilerParams(vmem_limit_bytes=SCOPED),
        cost_estimate=pl.CostEstimate(flops=2**22, bytes_accessed=6 * 2**20, transcendentals=0),
        name="encode",
    )(*(pltpu.with_memory_space_constraint(x, pltpu.HBM) for x in (weights, local, exponents, momentum)))
    return outs[:SIDE], outs[SIDE : 2 * SIDE], outs[2 * SIDE]


def squares_kernel(values, out):
    total = None
    for r in range(0, values.shape[0], 8):
        value = values[r : r + 8, :]
        total = value * value if total is None else total + value * value
    out[...] = total


def sum_squares(values):
    return pl.pallas_call(
        squares_kernel,
        out_shape=jax.ShapeDtypeStruct((8, WIDTH), jnp.float32),
        in_specs=[VMEM],
        out_specs=VMEM,
        compiler_params=pltpu.CompilerParams(vmem_limit_bytes=SCOPED),
        cost_estimate=pl.CostEstimate(flops=2**18, bytes_accessed=2**12, transcendentals=0),
        name="squares",
    )(values)


def update_kernel(threshold, *refs):
    mine, handed, (momentum, new_momentum, out, buf, sem) = refs[:5], refs[5:13], refs[13:]
    rows = momentum.shape[0]
    size, half = SIDE * rows, rows // 2
    me = lax.axis_index("replica")
    core = lax.rem(me, 2)
    squares = mine[-1][size:, :] + handed[-1][size:, :]
    magnitude = jnp.sqrt(jnp.sum(squares, axis=(0, 1), keepdims=True))
    factor = jnp.minimum(1.0, threshold / (magnitude + 1e-06))
    rate = OUTER_RATE * (1.0 + OUTER_MOMENTUM) * factor
    own = [(k, mine[n], 0, mine[n], size) for n, k in enumerate((0, 1, 3))]
    own.append((2, mine[3], 0, mine[4], 0))
    other = [(k, handed[2 * n], 0, handed[2 * n + 1], 0) for n, k in enumerate((0, 1, 3, 2))]
    copies = []
    for side, sources in ((core, own), (1 - core, other)):
        major, minor = axes_of(me, side)
        for k, averages, first, bases, offset in sources:
            place = lax.rem(major + SIDE - k, SIDE)
            for j in range(SIDE):
                apart = minor ^ j
                low = jnp.where(apart < 2, apart, 5 - apart)
                high = jnp.where(apart == 0, 0, lax.rem(apart, SIDE - 1) + 1)
                at = len(copies)
                for n, slot in enumerate((low, SIDE + high)):
                    base = pl.ds(pl.multiple_of(offset + slot * half, half), half)
                    average = averages[first + j * rows + n * half : first + j * rows + (n + 1) * half, :]
                    buf[at, n * half : (n + 1) * half, :] = bases[base, :] - rate * average
                columns = columns_of(owner_of(side, place, j))
                copy = pltpu.make_async_copy(buf.at[at], out.at[:, columns], sem.at[at])
                copy.start()
                copies.append(copy)
    here = pl.ds(pl.multiple_of(axes_of(me, core)[1] * rows, rows), rows)
    new_momentum[...] = OUTER_MOMENTUM * momentum[...] + factor * mine[0][here, :]
    for copy in copies:
        copy.wait()


def update(cols, threshold, mine, handed, momentum):
    rows = momentum.shape[0]
    chunks = 2 * SIDE * SIDE
    return pl.pallas_call(
        functools.partial(update_kernel, threshold),
        out_shape=[
            jax.ShapeDtypeStruct((rows, WIDTH), jnp.float32),
            jax.ShapeDtypeStruct((rows, cols), jnp.float32),
        ],
        in_specs=[VMEM] * (len(mine) + len(handed) + 1),
        out_specs=[VMEM, HBM],
        scratch_shapes=[
            pltpu.VMEM((chunks, rows, WIDTH), jnp.float32),
            pltpu.SemaphoreType.DMA((chunks,)),
        ],
        compiler_params=pltpu.CompilerParams(vmem_limit_bytes=SCOPED),
        cost_estimate=pl.CostEstimate(flops=2**21, bytes_accessed=2**22, transcendentals=0),
        name="update",
    )(*mine, *handed, momentum)


def tie(*values):
    return lax.optimization_barrier(values)


def per_device(global_weights, replica_weights, exponents, momentum):
    replica_count = lax.axis_size("replica")
    row_count, col_count = global_weights.shape
    threshold = CLIP_SCALE * math.sqrt(row_count * lax.axis_size("fsdp") * col_count)
    up, down = major_shift(1), major_shift(-1)

    def move(value, perm):
        return lax.ppermute(value, "replica", perm)

    with jax.named_scope("core_sum"):
        send, keep, base = encode(global_weights, replica_weights[0], exponents[0].T, momentum)
        parts = [kept + move(sent, CORE_SWAP) for sent, kept in zip(send, keep)]

    with jax.named_scope("major_sum"):
        arrived = [move(part, major_shift(k)) for part, k in zip(parts, STEPS)]
        total = parts[SIDE - 1] + arrived[0] + arrived[1] + arrived[2]
        low, high = total[:2], total[2:]

    with jax.named_scope("minor_sum"):
        size = low.shape[0] * row_count
        low, high = low.reshape(size, WIDTH), high.reshape(size, WIDTH)
        low_base, high_base = base[: row_count // 2], base[row_count // 2 :]
        for low_perm, high_perm in ((EVEN_PAIRS, ODD_PAIRS), (ODD_PAIRS, EVEN_PAIRS)):
            low_moved = move(jnp.concatenate([low, low_base]), low_perm)
            high_moved = move(jnp.concatenate([high, high_base]), high_perm)
            low, low_base = low + low_moved[:size], jnp.concatenate([low_base, low_moved[size:]])
            high, high_base = high + high_moved[:size], jnp.concatenate([high_base, high_moved[size:]])
        averages = jnp.concatenate([low, high]) / replica_count
        mine = jnp.concatenate([averages, low_base, high_base])
        middle = averages.shape[0]

    with jax.named_scope("square_sum"):
        squares = sum_squares(averages)
        squares = squares + lax.ppermute(squares, "fsdp", Z_ROUNDS[0])
        for perm in Z_ROUNDS[1:]:
            squares = squares + lax.ppermute(squares, "fsdp", perm)

    with jax.named_scope("major_gather"):
        below, above = move(mine, up), move(mine, down)

    with jax.named_scope("major_forward"):
        below, above, squares = tie(below, above, squares)
        far_low = move(jnp.concatenate([below[:middle], squares]), up)
        far_high = move(jnp.concatenate([above[middle:], squares]), down)

    with jax.named_scope("core_gather"):
        whole = tie(mine, squares)[0], below, above
        near = [move(part, CORE_SWAP) for x in whole for part in (x[:middle], x[middle:])]

    with jax.named_scope("square_sum"):
        across = move(squares, major_shift(2))
        far_low, far_high, near = tie(far_low, far_high, near)
        squares = squares + across + far_low[middle:] + far_high[middle:]

    with jax.named_scope("update"):
        (far_low,) = tie(far_low[:middle])
        far_high = jnp.concatenate([far_high[:middle], squares])
        handed = [*near, move(far_low, CORE_SWAP), move(far_high, CORE_SWAP)]
        new_momentum, new_weights = update(
            col_count, threshold, [mine, below, above, far_low, far_high], handed, momentum
        )
    return (new_weights, new_momentum)


def solution(mesh):
    in_specs = (
        P("fsdp", None),
        P("replica", "fsdp", None),
        P("replica", "fsdp", None),
        P("fsdp", "replica"),
    )
    out_specs = (P("fsdp", None), P("fsdp", "replica"))
    return jax.shard_map(
        per_device, mesh=mesh, in_specs=in_specs, out_specs=out_specs, check_vma=False
    )
```

```python
import functools
import math

import jax
import jax.numpy as jnp
from jax import lax
from jax.experimental import pallas as pl
from jax.experimental.pallas import tpu as pltpu
from jax.sharding import PartitionSpec as P

BLOCK = 128
SIDE = 4
WIDTH = 256
LOADS = 2
GROUPS = 4
STEPS = (2, 1, 3)

FP8_LIMIT = 448.0
CLIP_SCALE = 0.03
OUTER_RATE = 0.7
OUTER_MOMENTUM = 0.9

VMEM = pl.BlockSpec(memory_space=pltpu.VMEM)
HBM = pl.BlockSpec(memory_space=pltpu.HBM)
SCOPED = 12 * 1024 * 1024


def index_of(y, x, core):
    return (y % SIDE) * 8 + (x % SIDE) * 2 + core


def replica_perm(move):
    return [
        (index_of(y, x, core), index_of(*move(y, x, core)))
        for y in range(SIDE)
        for x in range(SIDE)
        for core in range(2)
    ]


def along_major(move):
    return replica_perm(lambda y, x, c: (y, move(x), c) if c == 0 else (move(y), x, c))


def along_minor(move):
    return replica_perm(lambda y, x, c: (move(y), x, c) if c == 0 else (y, move(x), c))


def major_shift(step):
    return along_major(lambda at: at + step)


def minor_shift(step):
    return along_minor(lambda at: at + step)


CORE_SWAP = replica_perm(lambda y, x, c: (y, x, 1 - c))
EVEN_PAIRS = along_minor(lambda at: at ^ 1)
ODD_PAIRS = along_minor(lambda at: ((at + 3) % 4 ^ 1) + 1)
Z_ROUNDS = [
    [(z, z ^ 1) for z in range(8)],
    [(z, z ^ 2) for z in range(8)],
    [(z, 7 - z) for z in range(8)],
]


def axes_of(me, core):
    x, y = lax.rem(me // 2, SIDE), me // 8
    return jnp.where(core == 0, x, y), jnp.where(core == 0, y, x)


def owner_of(core, major, minor):
    x, y = jnp.where(core == 0, major, minor), jnp.where(core == 0, minor, major)
    return y * 8 + x * 2 + core


def columns_of(owner):
    return pl.ds(pl.multiple_of(owner * WIDTH, WIDTH), WIDTH)


def encode_kernel(weights, local, exponents, momentum, *refs):
    outs, scratch = refs[: 2 * SIDE], refs[2 * SIDE :]
    base, wbuf, lbuf, ebuf, mbuf, limits, wsem, lsem, sem = scratch
    rows = weights.shape[0] // LOADS
    me = lax.axis_index("replica")
    core = lax.rem(me, 2)
    load_exponents = pltpu.make_async_copy(exponents, ebuf, sem.at[0])
    load_exponents.start()
    loads = []
    for n in range(LOADS):
        part = pl.ds(n * rows, rows)
        pair = (
            pltpu.make_async_copy(weights.at[part], wbuf.at[part], wsem.at[n]),
            pltpu.make_async_copy(local.at[part], lbuf.at[part], lsem.at[n]),
        )
        for copy in pair:
            copy.start()
        loads.append(pair)
    load_momentum = pltpu.make_async_copy(momentum, mbuf, sem.at[1])
    load_momentum.start()
    load_exponents.wait()
    tops = (FP8_LIMIT * jnp.exp2(ebuf[...].astype(jnp.float32))).astype(jnp.bfloat16)
    blocks = tops.shape[0]
    row = lax.broadcasted_iota(jnp.int32, (blocks, WIDTH), 0)
    col = lax.broadcasted_iota(jnp.int32, (blocks, WIDTH), 1) // BLOCK
    work = []
    for n, k in enumerate((*STEPS, 0)):
        for keep in range(2):
            for j in range(SIDE):
                target = core if keep else 1 - core
                owner = owner_of(target, lax.rem(axes_of(me, target)[0] + k, SIDE), j)
                pick = jnp.where(row == 2 * owner + col, 1.0, 0.0).astype(jnp.bfloat16)
                limits[len(work)] = lax.dot_general(
                    tops, pick, (((0,), (0,)), ((), ())), preferred_element_type=jnp.float32
                )
                work.append((outs[SIDE * keep + n], j, columns_of(owner)))
    for n in range(LOADS):
        for copy in loads[n]:
            copy.wait()
        part = pl.ds(n * rows, rows)
        for at, (out, slot, columns) in enumerate(work):
            limit = limits[at, part, :]
            difference = wbuf[part, columns] - lbuf[part, columns].astype(jnp.float32)
            out[slot, part, :] = jnp.clip(difference, -limit, limit)
    decay = OUTER_RATE * OUTER_MOMENTUM * OUTER_MOMENTUM
    load_momentum.wait()
    base[...] = wbuf[:, columns_of(me)] - decay * mbuf[...]


def encode(weights, local, exponents, momentum):
    rows, cols = weights.shape
    blocks = [jax.ShapeDtypeStruct((SIDE, rows, WIDTH), jnp.float32)] * SIDE
    outs = pl.pallas_call(
        encode_kernel,
        out_shape=[*blocks, *blocks, jax.ShapeDtypeStruct((rows, WIDTH), jnp.float32)],
        in_specs=[HBM] * 4,
        out_specs=[VMEM] * (2 * SIDE + 1),
        scratch_shapes=[
            pltpu.VMEM((rows, cols), jnp.float32),
            pltpu.VMEM((rows, cols), jnp.bfloat16),
            pltpu.VMEM(exponents.shape, jnp.int32),
            pltpu.VMEM(momentum.shape, jnp.float32),
            pltpu.VMEM((2 * SIDE * SIDE, rows, WIDTH), jnp.float32),
            pltpu.SemaphoreType.DMA((LOADS,)),
            pltpu.SemaphoreType.DMA((LOADS,)),
            pltpu.SemaphoreType.DMA((2,)),
        ],
        compiler_params=pltpu.CompilerParams(vmem_limit_bytes=SCOPED),
        cost_estimate=pl.CostEstimate(flops=2**22, bytes_accessed=6 * 2**20, transcendentals=0),
        name="encode",
    )(*(pltpu.with_memory_space_constraint(x, pltpu.HBM) for x in (weights, local, exponents, momentum)))
    return outs[:SIDE], outs[SIDE : 2 * SIDE], outs[2 * SIDE]


def squares_kernel(values, out):
    total = None
    for r in range(0, values.shape[0], 8):
        value = values[r : r + 8, :]
        total = value * value if total is None else total + value * value
    out[...] = total


def sum_squares(values):
    return pl.pallas_call(
        squares_kernel,
        out_shape=jax.ShapeDtypeStruct((8, WIDTH), jnp.float32),
        in_specs=[VMEM],
        out_specs=VMEM,
        compiler_params=pltpu.CompilerParams(vmem_limit_bytes=SCOPED),
        cost_estimate=pl.CostEstimate(flops=2**18, bytes_accessed=2**12, transcendentals=0),
        name="squares",
    )(values)


def update_kernel(threshold, *refs):
    mine, handed, (momentum, new_momentum, out, buf, sem) = refs[:5], refs[5:13], refs[13:]
    rows = momentum.shape[0]
    size, half = SIDE * rows, rows // 2
    me = lax.axis_index("replica")
    core = lax.rem(me, 2)
    squares = mine[-1][size:, :] + handed[-1][size:, :]
    magnitude = jnp.sqrt(jnp.sum(squares, axis=(0, 1), keepdims=True))
    factor = jnp.minimum(1.0, threshold / (magnitude + 1e-06))
    rate = OUTER_RATE * (1.0 + OUTER_MOMENTUM) * factor
    own = [(k, mine[n], 0, mine[n], size) for n, k in enumerate((0, 1, 3))]
    own.append((2, mine[3], 0, mine[4], 0))
    other = [(k, handed[2 * n], 0, handed[2 * n + 1], 0) for n, k in enumerate((0, 1, 3, 2))]
    work = []
    for side, sources in ((core, own), (1 - core, other)):
        major, minor = axes_of(me, side)
        for k, averages, first, bases, offset in sources:
            place = lax.rem(major + SIDE - k, SIDE)
            for j in range(SIDE):
                apart = minor ^ j
                low = jnp.where(apart < 2, apart, 5 - apart)
                high = jnp.where(apart == 0, 0, lax.rem(apart, SIDE - 1) + 1)
                places = offset + low * half, offset + (SIDE + high) * half
                work.append((averages, first + j * rows, bases, places, columns_of(owner_of(side, place, j))))
    copies = []
    group = rows // GROUPS
    for g in range(GROUPS):
        top = g * group
        part = pl.ds(top, group)
        for averages, first, bases, places, columns in work:
            start = places[top // half] + top % half
            base = bases[pl.ds(pl.multiple_of(start, group), group), :]
            buf[part, columns] = base - rate * averages[first + top : first + top + group, :]
        copy = pltpu.make_async_copy(buf.at[part], out.at[part], sem.at[g])
        copy.start()
        copies.append(copy)
    here = pl.ds(pl.multiple_of(axes_of(me, core)[1] * rows, rows), rows)
    new_momentum[...] = OUTER_MOMENTUM * momentum[...] + factor * mine[0][here, :]
    for copy in copies:
        copy.wait()


def update(cols, threshold, mine, handed, momentum):
    rows = momentum.shape[0]
    return pl.pallas_call(
        functools.partial(update_kernel, threshold),
        out_shape=[
            jax.ShapeDtypeStruct((rows, WIDTH), jnp.float32),
            jax.ShapeDtypeStruct((rows, cols), jnp.float32),
        ],
        in_specs=[VMEM] * (len(mine) + len(handed) + 1),
        out_specs=[VMEM, HBM],
        scratch_shapes=[
            pltpu.VMEM((rows, cols), jnp.float32),
            pltpu.SemaphoreType.DMA((GROUPS,)),
        ],
        compiler_params=pltpu.CompilerParams(vmem_limit_bytes=SCOPED),
        cost_estimate=pl.CostEstimate(flops=2**21, bytes_accessed=2**22, transcendentals=0),
        name="update",
    )(*mine, *handed, momentum)


def tie(*values):
    return lax.optimization_barrier(values)


def per_device(global_weights, replica_weights, exponents, momentum):
    replica_count = lax.axis_size("replica")
    row_count, col_count = global_weights.shape
    threshold = CLIP_SCALE * math.sqrt(row_count * lax.axis_size("fsdp") * col_count)
    up, down = major_shift(1), major_shift(-1)

    def move(value, perm):
        return lax.ppermute(value, "replica", perm)

    with jax.named_scope("core_sum"):
        send, keep, base = encode(global_weights, replica_weights[0], exponents[0].T, momentum)
        parts = [kept + move(sent, CORE_SWAP) for sent, kept in zip(send, keep)]

    with jax.named_scope("major_sum"):
        arrived = [move(part, major_shift(k)) for part, k in zip(parts, STEPS)]
        total = parts[SIDE - 1] + arrived[0] + arrived[1] + arrived[2]
        low, high = total[:2], total[2:]

    with jax.named_scope("minor_sum"):
        size = low.shape[0] * row_count
        low, high = low.reshape(size, WIDTH), high.reshape(size, WIDTH)
        low_base, high_base = base[: row_count // 2], base[row_count // 2 :]
        for low_perm, high_perm in ((EVEN_PAIRS, ODD_PAIRS), (ODD_PAIRS, EVEN_PAIRS)):
            low_moved = move(jnp.concatenate([low, low_base]), low_perm)
            high_moved = move(jnp.concatenate([high, high_base]), high_perm)
            low, low_base = low + low_moved[:size], jnp.concatenate([low_base, low_moved[size:]])
            high, high_base = high + high_moved[:size], jnp.concatenate([high_base, high_moved[size:]])
        averages = jnp.concatenate([low, high]) / replica_count
        mine = jnp.concatenate([averages, low_base, high_base])
        middle = averages.shape[0]

    with jax.named_scope("square_sum"):
        squares = sum_squares(averages)
        squares = squares + lax.ppermute(squares, "fsdp", Z_ROUNDS[0])
        for perm in Z_ROUNDS[1:]:
            squares = squares + lax.ppermute(squares, "fsdp", perm)

    with jax.named_scope("major_gather"):
        below, above = move(mine, up), move(mine, down)

    with jax.named_scope("major_forward"):
        below, above, squares = tie(below, above, squares)
        far_low = move(jnp.concatenate([below[:middle], squares]), up)
        far_high = move(jnp.concatenate([above[middle:], squares]), down)

    with jax.named_scope("core_gather"):
        whole = tie(mine, squares)[0], below, above
        near = [move(part, CORE_SWAP) for x in whole for part in (x[:middle], x[middle:])]

    with jax.named_scope("square_sum"):
        across = move(squares, major_shift(2))
        far_low, far_high, near = tie(far_low, far_high, near)
        squares = squares + across + far_low[middle:] + far_high[middle:]

    with jax.named_scope("update"):
        (far_low,) = tie(far_low[:middle])
        far_high = jnp.concatenate([far_high[:middle], squares])
        handed = [*near, move(far_low, CORE_SWAP), move(far_high, CORE_SWAP)]
        new_momentum, new_weights = update(
            col_count, threshold, [mine, below, above, far_low, far_high], handed, momentum
        )
    return (new_weights, new_momentum)


def solution(mesh):
    in_specs = (
        P("fsdp", None),
        P("replica", "fsdp", None),
        P("replica", "fsdp", None),
        P("fsdp", "replica"),
    )
    out_specs = (P("fsdp", None), P("fsdp", "replica"))
    return jax.shard_map(
        per_device, mesh=mesh, in_specs=in_specs, out_specs=out_specs, check_vma=False
    )
```

```python
import functools
import math

import jax
import jax.numpy as jnp
from jax import lax
from jax.experimental import pallas as pl
from jax.experimental.pallas import tpu as pltpu
from jax.sharding import PartitionSpec as P

BLOCK = 128
SIDE = 4
WIDTH = 256
LOADS = 2
GROUPS = 4
STEPS = (2, 1, 3)

FP8_LIMIT = 448.0
CLIP_SCALE = 0.03
OUTER_RATE = 0.7
OUTER_MOMENTUM = 0.9

VMEM = pl.BlockSpec(memory_space=pltpu.VMEM)
HBM = pl.BlockSpec(memory_space=pltpu.HBM)
SCOPED = 12 * 1024 * 1024


def index_of(y, x, core):
    return (y % SIDE) * 8 + (x % SIDE) * 2 + core


def replica_perm(move):
    return [
        (index_of(y, x, core), index_of(*move(y, x, core)))
        for y in range(SIDE)
        for x in range(SIDE)
        for core in range(2)
    ]


def along_major(move):
    return replica_perm(lambda y, x, c: (y, move(x), c) if c == 0 else (move(y), x, c))


def along_minor(move):
    return replica_perm(lambda y, x, c: (move(y), x, c) if c == 0 else (y, move(x), c))


def major_shift(step):
    return along_major(lambda at: at + step)


def minor_shift(step):
    return along_minor(lambda at: at + step)


CORE_SWAP = replica_perm(lambda y, x, c: (y, x, 1 - c))
EVEN_PAIRS = along_minor(lambda at: at ^ 1)
ODD_PAIRS = along_minor(lambda at: ((at + 3) % 4 ^ 1) + 1)
Z_ROUNDS = [
    [(z, z ^ 1) for z in range(8)],
    [(z, z ^ 2) for z in range(8)],
    [(z, 7 - z) for z in range(8)],
]


def axes_of(me, core):
    x, y = lax.rem(me // 2, SIDE), me // 8
    return jnp.where(core == 0, x, y), jnp.where(core == 0, y, x)


def owner_of(core, major, minor):
    x, y = jnp.where(core == 0, major, minor), jnp.where(core == 0, minor, major)
    return y * 8 + x * 2 + core


def columns_of(owner):
    return pl.ds(pl.multiple_of(owner * WIDTH, WIDTH), WIDTH)


def encode_kernel(weights, local, exponents, momentum, *refs):
    outs, scratch = refs[: 2 * SIDE], refs[2 * SIDE :]
    base, wbuf, lbuf, ebuf, mbuf, limits, wsem, lsem, sem = scratch
    rows = weights.shape[0] // LOADS
    me = lax.axis_index("replica")
    core = lax.rem(me, 2)
    load_exponents = pltpu.make_async_copy(exponents, ebuf, sem.at[0])
    load_exponents.start()
    loads = []
    for n in range(LOADS):
        part = pl.ds(n * rows, rows)
        pair = (
            pltpu.make_async_copy(weights.at[part], wbuf.at[part], wsem.at[n]),
            pltpu.make_async_copy(local.at[part], lbuf.at[part], lsem.at[n]),
        )
        for copy in pair:
            copy.start()
        loads.append(pair)
    load_momentum = pltpu.make_async_copy(momentum, mbuf, sem.at[1])
    load_momentum.start()
    load_exponents.wait()
    tops = (FP8_LIMIT * jnp.exp2(ebuf[...].astype(jnp.float32))).astype(jnp.bfloat16)
    blocks = tops.shape[0]
    row = lax.broadcasted_iota(jnp.int32, (blocks, WIDTH), 0)
    col = lax.broadcasted_iota(jnp.int32, (blocks, WIDTH), 1) // BLOCK
    work = []
    for n, k in enumerate((*STEPS, 0)):
        for keep in range(2):
            for j in range(SIDE):
                target = core if keep else 1 - core
                owner = owner_of(target, lax.rem(axes_of(me, target)[0] + k, SIDE), j)
                pick = jnp.where(row == 2 * owner + col, 1.0, 0.0).astype(jnp.bfloat16)
                limits[len(work)] = lax.dot_general(
                    tops, pick, (((0,), (0,)), ((), ())), preferred_element_type=jnp.float32
                )
                work.append((outs[SIDE * keep + n], j, columns_of(owner)))
    for n in range(LOADS):
        for copy in loads[n]:
            copy.wait()
        part = pl.ds(n * rows, rows)
        for at, (out, slot, columns) in enumerate(work):
            limit = limits[at, part, :]
            difference = wbuf[part, columns] - lbuf[part, columns].astype(jnp.float32)
            out[slot, part, :] = jnp.clip(difference, -limit, limit)
    decay = OUTER_RATE * OUTER_MOMENTUM * OUTER_MOMENTUM
    load_momentum.wait()
    base[...] = wbuf[:, columns_of(me)] - decay * mbuf[...]


def encode(weights, local, exponents, momentum):
    rows, cols = weights.shape
    blocks = [jax.ShapeDtypeStruct((SIDE, rows, WIDTH), jnp.float32)] * SIDE
    outs = pl.pallas_call(
        encode_kernel,
        out_shape=[*blocks, *blocks, jax.ShapeDtypeStruct((rows, WIDTH), jnp.float32)],
        in_specs=[HBM] * 4,
        out_specs=[VMEM] * (2 * SIDE + 1),
        scratch_shapes=[
            pltpu.VMEM((rows, cols), jnp.float32),
            pltpu.VMEM((rows, cols), jnp.bfloat16),
            pltpu.VMEM(exponents.shape, jnp.int32),
            pltpu.VMEM(momentum.shape, jnp.float32),
            pltpu.VMEM((2 * SIDE * SIDE, rows, WIDTH), jnp.float32),
            pltpu.SemaphoreType.DMA((LOADS,)),
            pltpu.SemaphoreType.DMA((LOADS,)),
            pltpu.SemaphoreType.DMA((2,)),
        ],
        compiler_params=pltpu.CompilerParams(vmem_limit_bytes=SCOPED),
        cost_estimate=pl.CostEstimate(flops=2**22, bytes_accessed=6 * 2**20, transcendentals=0),
        name="encode",
    )(*(pltpu.with_memory_space_constraint(x, pltpu.HBM) for x in (weights, local, exponents, momentum)))
    return outs[:SIDE], outs[SIDE : 2 * SIDE], outs[2 * SIDE]


def squares_kernel(values, out):
    total = None
    for r in range(0, values.shape[0], 8):
        value = values[r : r + 8, :]
        total = value * value if total is None else total + value * value
    out[...] = total


def sum_squares(values):
    return pl.pallas_call(
        squares_kernel,
        out_shape=jax.ShapeDtypeStruct((8, WIDTH), jnp.float32),
        in_specs=[VMEM],
        out_specs=VMEM,
        compiler_params=pltpu.CompilerParams(vmem_limit_bytes=SCOPED),
        cost_estimate=pl.CostEstimate(flops=2**18, bytes_accessed=2**12, transcendentals=0),
        name="squares",
    )(values)


def update_kernel(threshold, *refs):
    mine, handed, (momentum, new_momentum, out, buf, sem) = refs[:5], refs[5:13], refs[13:]
    rows = momentum.shape[0]
    size, half = SIDE * rows, rows // 2
    me = lax.axis_index("replica")
    core = lax.rem(me, 2)
    squares = mine[-1][size:, :] + handed[-1][size:, :]
    magnitude = jnp.sqrt(jnp.sum(squares, axis=(0, 1), keepdims=True))
    factor = jnp.minimum(1.0, threshold / (magnitude + 1e-06))
    rate = OUTER_RATE * (1.0 + OUTER_MOMENTUM) * factor
    own = [(k, mine[n], 0, mine[n], size) for n, k in enumerate((0, 1, 3))]
    own.append((2, mine[3], 0, mine[4], 0))
    other = [(k, handed[2 * n], 0, handed[2 * n + 1], 0) for n, k in enumerate((0, 1, 3, 2))]
    work = []
    for side, sources in ((core, own), (1 - core, other)):
        major, minor = axes_of(me, side)
        for k, averages, first, bases, offset in sources:
            place = lax.rem(major + SIDE - k, SIDE)
            for j in range(SIDE):
                apart = minor ^ j
                low = jnp.where(apart < 2, apart, 5 - apart)
                high = jnp.where(apart == 0, 0, lax.rem(apart, SIDE - 1) + 1)
                places = offset + low * half, offset + (SIDE + high) * half
                work.append((averages, first + j * rows, bases, places, columns_of(owner_of(side, place, j))))
    copies = []
    group = rows // GROUPS
    for g in range(GROUPS):
        top = g * group
        part = pl.ds(top, group)
        for averages, first, bases, places, columns in work:
            start = places[top // half] + top % half
            base = bases[pl.ds(pl.multiple_of(start, group), group), :]
            buf[part, columns] = base - rate * averages[first + top : first + top + group, :]
        copy = pltpu.make_async_copy(buf.at[part], out.at[part], sem.at[g])
        copy.start()
        copies.append(copy)
    here = pl.ds(pl.multiple_of(axes_of(me, core)[1] * rows, rows), rows)
    new_momentum[...] = OUTER_MOMENTUM * momentum[...] + factor * mine[0][here, :]
    for copy in copies:
        copy.wait()


def update(cols, threshold, mine, handed, momentum):
    rows = momentum.shape[0]
    return pl.pallas_call(
        functools.partial(update_kernel, threshold),
        out_shape=[
            jax.ShapeDtypeStruct((rows, WIDTH), jnp.float32),
            jax.ShapeDtypeStruct((rows, cols), jnp.float32),
        ],
        in_specs=[VMEM] * (len(mine) + len(handed) + 1),
        out_specs=[VMEM, HBM],
        scratch_shapes=[
            pltpu.VMEM((rows, cols), jnp.float32),
            pltpu.SemaphoreType.DMA((GROUPS,)),
        ],
        compiler_params=pltpu.CompilerParams(vmem_limit_bytes=SCOPED),
        cost_estimate=pl.CostEstimate(flops=2**21, bytes_accessed=2**22, transcendentals=0),
        name="update",
    )(*mine, *handed, momentum)


def tie(*values):
    return lax.optimization_barrier(values)


def per_device(global_weights, replica_weights, exponents, momentum):
    replica_count = lax.axis_size("replica")
    row_count, col_count = global_weights.shape
    threshold = CLIP_SCALE * math.sqrt(row_count * lax.axis_size("fsdp") * col_count)
    up, down = major_shift(1), major_shift(-1)

    def move(value, perm):
        return lax.ppermute(value, "replica", perm)

    with jax.named_scope("core_sum"):
        send, keep, base = encode(global_weights, replica_weights[0], exponents[0].T, momentum)
        first = move(send[0], CORE_SWAP)
        first, *others = tie(first, *send[1:])
        parts = [kept + sent for sent, kept in zip((first, *(move(x, CORE_SWAP) for x in others)), keep)]

    with jax.named_scope("major_sum"):
        arrived = [move(part, major_shift(k)) for part, k in zip(parts, STEPS)]
        total = parts[SIDE - 1] + arrived[0] + arrived[1] + arrived[2]
        low, high = total[:2], total[2:]

    with jax.named_scope("minor_sum"):
        size = low.shape[0] * row_count
        low, high = low.reshape(size, WIDTH), high.reshape(size, WIDTH)
        low_base, high_base = base[: row_count // 2], base[row_count // 2 :]
        for low_perm, high_perm in ((EVEN_PAIRS, ODD_PAIRS), (ODD_PAIRS, EVEN_PAIRS)):
            low_moved = move(jnp.concatenate([low, low_base]), low_perm)
            high_moved = move(jnp.concatenate([high, high_base]), high_perm)
            low, low_base = low + low_moved[:size], jnp.concatenate([low_base, low_moved[size:]])
            high, high_base = high + high_moved[:size], jnp.concatenate([high_base, high_moved[size:]])
        averages = jnp.concatenate([low, high]) / replica_count
        mine = jnp.concatenate([averages, low_base, high_base])
        middle = averages.shape[0]

    with jax.named_scope("square_sum"):
        squares = sum_squares(averages)
        squares = squares + lax.ppermute(squares, "fsdp", Z_ROUNDS[0])
        for perm in Z_ROUNDS[1:]:
            squares = squares + lax.ppermute(squares, "fsdp", perm)

    with jax.named_scope("major_gather"):
        below, above = move(mine, up), move(mine, down)

    with jax.named_scope("major_forward"):
        below, above, squares = tie(below, above, squares)
        far_low = move(jnp.concatenate([below[:middle], squares]), up)
        far_high = move(jnp.concatenate([above[middle:], squares]), down)

    with jax.named_scope("core_gather"):
        whole = tie(mine, squares)[0], below, above
        near = [move(part, CORE_SWAP) for x in whole for part in (x[:middle], x[middle:])]

    with jax.named_scope("square_sum"):
        across = move(squares, major_shift(2))
        far_low, far_high, near = tie(far_low, far_high, near)
        squares = squares + across + far_low[middle:] + far_high[middle:]

    with jax.named_scope("update"):
        (far_low,) = tie(far_low[:middle])
        far_high = jnp.concatenate([far_high[:middle], squares])
        handed = [*near, move(far_low, CORE_SWAP), move(far_high, CORE_SWAP)]
        new_momentum, new_weights = update(
            col_count, threshold, [mine, below, above, far_low, far_high], handed, momentum
        )
    return (new_weights, new_momentum)


def solution(mesh):
    in_specs = (
        P("fsdp", None),
        P("replica", "fsdp", None),
        P("replica", "fsdp", None),
        P("fsdp", "replica"),
    )
    out_specs = (P("fsdp", None), P("fsdp", "replica"))
    return jax.shard_map(
        per_device, mesh=mesh, in_specs=in_specs, out_specs=out_specs, check_vma=False
    )
```

```python
import functools
import math

import jax
import jax.numpy as jnp
from jax import lax
from jax.experimental import pallas as pl
from jax.experimental.pallas import tpu as pltpu
from jax.sharding import PartitionSpec as P

BLOCK = 128
SIDE = 4
WIDTH = 256
LOADS = 2
GROUPS = 4
STEPS = (2, 1, 3)

FP8_LIMIT = 448.0
CLIP_SCALE = 0.03
OUTER_RATE = 0.7
OUTER_MOMENTUM = 0.9

VMEM = pl.BlockSpec(memory_space=pltpu.VMEM)
HBM = pl.BlockSpec(memory_space=pltpu.HBM)
SCOPED = 12 * 1024 * 1024


def index_of(y, x, core):
    return (y % SIDE) * 8 + (x % SIDE) * 2 + core


def replica_perm(move):
    return [
        (index_of(y, x, core), index_of(*move(y, x, core)))
        for y in range(SIDE)
        for x in range(SIDE)
        for core in range(2)
    ]


def along_major(move):
    return replica_perm(lambda y, x, c: (y, move(x), c) if c == 0 else (move(y), x, c))


def along_minor(move):
    return replica_perm(lambda y, x, c: (move(y), x, c) if c == 0 else (y, move(x), c))


def major_shift(step):
    return along_major(lambda at: at + step)


def minor_shift(step):
    return along_minor(lambda at: at + step)


CORE_SWAP = replica_perm(lambda y, x, c: (y, x, 1 - c))
EVEN_PAIRS = along_minor(lambda at: at ^ 1)
ODD_PAIRS = along_minor(lambda at: ((at + 3) % 4 ^ 1) + 1)
Z_ROUNDS = [
    [(z, z ^ 1) for z in range(8)],
    [(z, z ^ 2) for z in range(8)],
    [(z, 7 - z) for z in range(8)],
]


def axes_of(me, core):
    x, y = lax.rem(me // 2, SIDE), me // 8
    return jnp.where(core == 0, x, y), jnp.where(core == 0, y, x)


def owner_of(core, major, minor):
    x, y = jnp.where(core == 0, major, minor), jnp.where(core == 0, minor, major)
    return y * 8 + x * 2 + core


def columns_of(owner):
    return pl.ds(pl.multiple_of(owner * WIDTH, WIDTH), WIDTH)


def encode_kernel(weights, local, exponents, momentum, *refs):
    outs, scratch = refs[: 2 * SIDE], refs[2 * SIDE :]
    base, wbuf, lbuf, ebuf, mbuf, limits, wsem, lsem, sem = scratch
    rows = weights.shape[0] // LOADS
    me = lax.axis_index("replica")
    core = lax.rem(me, 2)
    load_exponents = pltpu.make_async_copy(exponents, ebuf, sem.at[0])
    load_exponents.start()
    loads = []
    for n in range(LOADS):
        part = pl.ds(n * rows, rows)
        pair = (
            pltpu.make_async_copy(weights.at[part], wbuf.at[part], wsem.at[n]),
            pltpu.make_async_copy(local.at[part], lbuf.at[part], lsem.at[n]),
        )
        for copy in pair:
            copy.start()
        loads.append(pair)
    load_momentum = pltpu.make_async_copy(momentum, mbuf, sem.at[1])
    load_momentum.start()
    load_exponents.wait()
    tops = (FP8_LIMIT * jnp.exp2(ebuf[...].astype(jnp.float32))).astype(jnp.bfloat16)
    blocks = tops.shape[0]
    row = lax.broadcasted_iota(jnp.int32, (blocks, WIDTH), 0)
    col = lax.broadcasted_iota(jnp.int32, (blocks, WIDTH), 1) // BLOCK
    work = []
    for n, k in enumerate((*STEPS, 0)):
        for keep in range(2):
            for j in range(SIDE):
                target = core if keep else 1 - core
                owner = owner_of(target, lax.rem(axes_of(me, target)[0] + k, SIDE), j)
                pick = jnp.where(row == 2 * owner + col, 1.0, 0.0).astype(jnp.bfloat16)
                limits[len(work)] = lax.dot_general(
                    tops, pick, (((0,), (0,)), ((), ())), preferred_element_type=jnp.float32
                )
                work.append((outs[SIDE * keep + n], j, columns_of(owner)))
    for n in range(LOADS):
        for copy in loads[n]:
            copy.wait()
        part = pl.ds(n * rows, rows)
        for at, (out, slot, columns) in enumerate(work):
            limit = limits[at, part, :]
            difference = wbuf[part, columns] - lbuf[part, columns].astype(jnp.float32)
            out[slot, part, :] = jnp.clip(difference, -limit, limit)
    decay = OUTER_RATE * OUTER_MOMENTUM * OUTER_MOMENTUM
    load_momentum.wait()
    base[...] = wbuf[:, columns_of(me)] - decay * mbuf[...]


def encode(weights, local, exponents, momentum):
    rows, cols = weights.shape
    blocks = [jax.ShapeDtypeStruct((SIDE, rows, WIDTH), jnp.float32)] * SIDE
    outs = pl.pallas_call(
        encode_kernel,
        out_shape=[*blocks, *blocks, jax.ShapeDtypeStruct((rows, WIDTH), jnp.float32)],
        in_specs=[HBM] * 4,
        out_specs=[VMEM] * (2 * SIDE + 1),
        scratch_shapes=[
            pltpu.VMEM((rows, cols), jnp.float32),
            pltpu.VMEM((rows, cols), jnp.bfloat16),
            pltpu.VMEM(exponents.shape, jnp.int32),
            pltpu.VMEM(momentum.shape, jnp.float32),
            pltpu.VMEM((2 * SIDE * SIDE, rows, WIDTH), jnp.float32),
            pltpu.SemaphoreType.DMA((LOADS,)),
            pltpu.SemaphoreType.DMA((LOADS,)),
            pltpu.SemaphoreType.DMA((2,)),
        ],
        compiler_params=pltpu.CompilerParams(vmem_limit_bytes=SCOPED),
        cost_estimate=pl.CostEstimate(flops=2**22, bytes_accessed=6 * 2**20, transcendentals=0),
        name="encode",
    )(*(pltpu.with_memory_space_constraint(x, pltpu.HBM) for x in (weights, local, exponents, momentum)))
    return outs[:SIDE], outs[SIDE : 2 * SIDE], outs[2 * SIDE]


def squares_kernel(values, out):
    total = None
    for r in range(0, values.shape[0], 8):
        value = values[r : r + 8, :]
        total = value * value if total is None else total + value * value
    out[...] = total


def sum_squares(values):
    return pl.pallas_call(
        squares_kernel,
        out_shape=jax.ShapeDtypeStruct((8, WIDTH), jnp.float32),
        in_specs=[VMEM],
        out_specs=VMEM,
        compiler_params=pltpu.CompilerParams(vmem_limit_bytes=SCOPED),
        cost_estimate=pl.CostEstimate(flops=2**18, bytes_accessed=2**12, transcendentals=0),
        name="squares",
    )(values)


def update_kernel(threshold, *refs):
    mine, handed, (momentum, new_momentum, out, buf, sem) = refs[:5], refs[5:8], refs[8:]
    rows = momentum.shape[0]
    size, half = SIDE * rows, rows // 2
    me = lax.axis_index("replica")
    core = lax.rem(me, 2)
    squares = mine[-1][size:, :] + handed[-1][size:, :]
    magnitude = jnp.sqrt(jnp.sum(squares, axis=(0, 1), keepdims=True))
    factor = jnp.minimum(1.0, threshold / (magnitude + 1e-06))
    rate = OUTER_RATE * (1.0 + OUTER_MOMENTUM) * factor
    own = [(k, mine[n], 0, mine[n], size) for n, k in enumerate((0, 1, 3))]
    own.append((2, mine[3], 0, mine[4], 0))
    other = [(k, handed[0], 2 * n * size, handed[0], (2 * n + 1) * size) for n, k in enumerate((0, 1, 3))]
    other.append((2, handed[1], 0, handed[2], 0))
    work = []
    for side, sources in ((core, own), (1 - core, other)):
        major, minor = axes_of(me, side)
        for k, averages, first, bases, offset in sources:
            place = lax.rem(major + SIDE - k, SIDE)
            for j in range(SIDE):
                apart = minor ^ j
                low = jnp.where(apart < 2, apart, 5 - apart)
                high = jnp.where(apart == 0, 0, lax.rem(apart, SIDE - 1) + 1)
                places = offset + low * half, offset + (SIDE + high) * half
                work.append((averages, first + j * rows, bases, places, columns_of(owner_of(side, place, j))))
    copies = []
    group = rows // GROUPS
    for g in range(GROUPS):
        top = g * group
        part = pl.ds(top, group)
        for averages, first, bases, places, columns in work:
            start = places[top // half] + top % half
            base = bases[pl.ds(pl.multiple_of(start, group), group), :]
            buf[part, columns] = base - rate * averages[first + top : first + top + group, :]
        copy = pltpu.make_async_copy(buf.at[part], out.at[part], sem.at[g])
        copy.start()
        copies.append(copy)
    here = pl.ds(pl.multiple_of(axes_of(me, core)[1] * rows, rows), rows)
    new_momentum[...] = OUTER_MOMENTUM * momentum[...] + factor * mine[0][here, :]
    for copy in copies:
        copy.wait()


def update(cols, threshold, mine, handed, momentum):
    rows = momentum.shape[0]
    return pl.pallas_call(
        functools.partial(update_kernel, threshold),
        out_shape=[
            jax.ShapeDtypeStruct((rows, WIDTH), jnp.float32),
            jax.ShapeDtypeStruct((rows, cols), jnp.float32),
        ],
        in_specs=[VMEM] * (len(mine) + len(handed) + 1),
        out_specs=[VMEM, HBM],
        scratch_shapes=[
            pltpu.VMEM((rows, cols), jnp.float32),
            pltpu.SemaphoreType.DMA((GROUPS,)),
        ],
        compiler_params=pltpu.CompilerParams(vmem_limit_bytes=SCOPED),
        cost_estimate=pl.CostEstimate(flops=2**21, bytes_accessed=2**22, transcendentals=0),
        name="update",
    )(*mine, *handed, momentum)


def tie(*values):
    return lax.optimization_barrier(values)


def per_device(global_weights, replica_weights, exponents, momentum):
    replica_count = lax.axis_size("replica")
    row_count, col_count = global_weights.shape
    threshold = CLIP_SCALE * math.sqrt(row_count * lax.axis_size("fsdp") * col_count)
    up, down = major_shift(1), major_shift(-1)

    def move(value, perm):
        return lax.ppermute(value, "replica", perm)

    with jax.named_scope("core_sum"):
        send, keep, base = encode(global_weights, replica_weights[0], exponents[0].T, momentum)
        parts = [kept + move(sent, CORE_SWAP) for sent, kept in zip(send, keep)]

    with jax.named_scope("major_sum"):
        arrived = [move(part, major_shift(k)) for part, k in zip(parts, STEPS)]
        total = parts[SIDE - 1] + arrived[0] + arrived[1] + arrived[2]
        low, high = total[:2], total[2:]

    with jax.named_scope("minor_sum"):
        size = low.shape[0] * row_count
        low, high = low.reshape(size, WIDTH), high.reshape(size, WIDTH)
        low_base, high_base = base[: row_count // 2], base[row_count // 2 :]
        for low_perm, high_perm in ((EVEN_PAIRS, ODD_PAIRS), (ODD_PAIRS, EVEN_PAIRS)):
            low_moved = move(jnp.concatenate([low, low_base]), low_perm)
            high_moved = move(jnp.concatenate([high, high_base]), high_perm)
            low, low_base = low + low_moved[:size], jnp.concatenate([low_base, low_moved[size:]])
            high, high_base = high + high_moved[:size], jnp.concatenate([high_base, high_moved[size:]])
        averages = jnp.concatenate([low, high]) / replica_count
        mine = jnp.concatenate([averages, low_base, high_base])
        middle = averages.shape[0]

    with jax.named_scope("square_sum"):
        squares = sum_squares(averages)
        squares = squares + lax.ppermute(squares, "fsdp", Z_ROUNDS[0])
        for perm in Z_ROUNDS[1:]:
            squares = squares + lax.ppermute(squares, "fsdp", perm)

    with jax.named_scope("major_gather"):
        below, above = move(mine, up), move(mine, down)

    with jax.named_scope("major_forward"):
        below, above, squares = tie(below, above, squares)
        far_low = move(jnp.concatenate([below[:middle], squares]), up)
        far_high = move(jnp.concatenate([above[middle:], squares]), down)

    with jax.named_scope("core_gather"):
        near = move(jnp.concatenate([mine, below, above]), CORE_SWAP)

    with jax.named_scope("square_sum"):
        across = move(squares, major_shift(2))
        squares = squares + across + far_low[middle:] + far_high[middle:]

    with jax.named_scope("update"):
        (far_low,) = tie(far_low[:middle])
        far_high = jnp.concatenate([far_high[:middle], squares])
        handed = [near, move(far_low, CORE_SWAP), move(far_high, CORE_SWAP)]
        new_momentum, new_weights = update(
            col_count, threshold, [mine, below, above, far_low, far_high], handed, momentum
        )
    return (new_weights, new_momentum)


def solution(mesh):
    in_specs = (
        P("fsdp", None),
        P("replica", "fsdp", None),
        P("replica", "fsdp", None),
        P("fsdp", "replica"),
    )
    out_specs = (P("fsdp", None), P("fsdp", "replica"))
    return jax.shard_map(
        per_device, mesh=mesh, in_specs=in_specs, out_specs=out_specs, check_vma=False
    )
```
